32 devices in a mesh: grp: 2 (over y), param: 16 (over z, x, core).
Axes of the slice: x: 2, y: 2, z: 4, core: 2. Of those that a mesh axis runs over, the one named last changes fastest.
Arguments:
- basis_a: bfloat16 [8192, 8192], P('param'), may hold values from -0.0625 to 0.0625
- basis_g: bfloat16 [14336, 14336], P('param'), may hold values from -0.046875 to 0.046875
- query_a: bfloat16 [16, 32, 8192], P('grp', None, 'param'), parts along dimension 0, may hold values from -0.0625 to 0.0625
- query_g: bfloat16 [16, 32, 14336], P('grp', None, 'param'), parts along dimension 0, may hold values from -0.046875 to 0.046875
- acts: bfloat16 [6144, 8192], P(('grp', 'param')), parts along dimension 0, may hold values from -6 to 6
- grads: bfloat16 [6144, 14336], P(('grp', 'param')), parts along dimension 0, may hold values from -0.29882812 to 0.29882812
- cand_blocks: int32 [8, 4], P('grp'), parts along dimension 0, may hold values from 0 to 15, as said below
- cand_count: int32 [8], P('grp'), parts along dimension 0, may hold values from 1 to 4, as said below
Outputs:
- scores: float32 [16, 48], P('grp', 'param'), parts along dimension 0
- top_scores: float32 [16, 16], P('grp'), parts along dimension 0
The draws below stay inside these ranges and needn't reach their ends.
There are 2 independent parts, one for each index of `grp`. The reference program is written for one: setup_inputs(seed, part) draws one part's arguments, and reference() takes and returns one part's arrays. A program takes and returns all parts, laid end to end along the dimension named above; an argument that names none is the same for every part. Nothing has to cross between parts.
Inputs may be any that keep to these rules, and one draw needn't show every extreme that they name: `cand_blocks`: within a row the ids are distinct. Counting only the first cand_count slots of each row, every sequence block is listed by at most 2 query blocks, and some block by exactly 2. `cand_count`: some query block uses all 4 slots.
All inputs are finite; a program needn't handle non-finite values.
Results may differ from the reference program's by a relative error of at most 0.0045.
Values may be sent and summed in bfloat16 or wider, within the bound.
A program may use at most 192 MiB of HBM per device.

```python
import jax
import jax.numpy as jnp
from jax import lax

D = 8192
F = 14336
RANK = 32
QB = 2
NQB = 4
SEQ_LEN = 64
SEQ_DEV = 3
TOPK = 16
QUERIES = 8
NSB = 16
NSEQ = 48
TOKENS = 3072
MAXC = 4


def candidate_lists(key):
    order = jax.random.permutation(jax.random.fold_in(key, 11), NSB).astype(jnp.int32)
    counts = jax.random.randint(jax.random.fold_in(key, 12), (NQB,), 1, MAXC + 1).astype(jnp.int32)
    full_row = jax.random.randint(jax.random.fold_in(key, 13), (), 0, NQB - 1).astype(jnp.int32)
    counts = jnp.where(jnp.arange(NQB, dtype=jnp.int32) == full_row, MAXC, counts).astype(jnp.int32)
    offset = jnp.argmax(order == NSB - 1).astype(jnp.int32)
    starts = jnp.arange(NQB, dtype=jnp.int32) * (MAXC // 2)
    places = (offset + starts[:, None] + jnp.arange(MAXC, dtype=jnp.int32)[None, :]) % NSB
    return (order[places].astype(jnp.int32), counts)


def draw_cand_blocks(key, part):
    lists = candidate_lists(key)
    return lists[0]


def draw_cand_count(key, part):
    lists = candidate_lists(key)
    return lists[1]


def block_levels(key, extent, cuts, low, top_value):
    gain = 1.0
    for dim, blocks in cuts:
        draws = jax.random.uniform(jax.random.fold_in(jax.random.fold_in(key, 6), dim), (blocks,), jnp.float32, low / len(cuts), top_value / len(cuts))
        gain = gain * jnp.repeat(jnp.exp(draws), extent[dim] // blocks).reshape((-1,) + (1,) * (len(extent) - 1 - dim))
    return gain


def bell_draw(stream_key, shape, scale, reach, cuts=(), kind=jnp.bfloat16):
    values = scale * jax.random.normal(stream_key, shape, jnp.float32)
    if cuts:
        values = values * block_levels(stream_key, shape, cuts, -0.22, 0.18)
    return jnp.clip(values, -reach, reach).astype(kind)


def setup_inputs(seed: int = 0, part: int = 0) -> dict:
    seeds = jax.random.split(jax.random.key(seed), 9)
    part_splits = jax.random.split(jax.random.fold_in(seeds[8], part), 9)
    basis_a = bell_draw(seeds[0], (D, D), D ** -0.5, 0.0625, ((0, 16),))
    basis_g = bell_draw(seeds[1], (F, F), F ** -0.5, 0.046875, ((0, 16),))
    query_a = bell_draw(part_splits[2], (QUERIES, RANK, D), D ** -0.5, 0.0625, ((2, 16),))
    query_g = bell_draw(part_splits[3], (QUERIES, RANK, F), F ** -0.5, 0.046875, ((2, 16),))
    acts = bell_draw(part_splits[4], (TOKENS, D), 1.0, 6.0, ((0, 16),))
    grads = bell_draw(part_splits[5], (TOKENS, F), 0.05, 0.29882812, ((0, 16),))
    cand_blocks = draw_cand_blocks(jax.random.fold_in(jax.random.fold_in(seeds[8], part), 71), part)
    cand_count = draw_cand_count(jax.random.fold_in(jax.random.fold_in(seeds[8], part), 71), part)
    return dict(basis_a=basis_a, basis_g=basis_g, query_a=query_a, query_g=query_g, acts=acts, grads=grads, cand_blocks=cand_blocks, cand_count=cand_count)


def contract_last(left, right):
    return lax.dot_general(left, right, (((1,), (1,)), ((), ())), preferred_element_type=jnp.float32)


def reference(basis_a, basis_g, query_a, query_g, acts, grads, cand_blocks, cand_count):
    back_a = contract_last(query_a.reshape(QUERIES * RANK, D), basis_a).astype(jnp.bfloat16)
    back_g = contract_last(query_g.reshape(QUERIES * RANK, F), basis_g).astype(jnp.bfloat16)
    proj_a = contract_last(back_a, acts)
    proj_g = contract_last(back_g, grads)
    token_score = (proj_a * proj_g).reshape(QUERIES, RANK, TOKENS).sum(axis=1)
    seq_sums = token_score.reshape(QUERIES, NSEQ, SEQ_LEN).sum(axis=2)
    positions = jnp.arange(MAXC, dtype=jnp.int32)
    live_slot = positions[None, :] < cand_count[:, None]
    block_ids = jnp.arange(NSB, dtype=jnp.int32)
    listed = jnp.sum((live_slot[:, :, None] & (cand_blocks[:, :, None] == block_ids[None, None, :])).astype(jnp.int32), axis=1)
    query_block = jnp.arange(QUERIES, dtype=jnp.int32) // QB
    seq_block = jnp.arange(NSEQ, dtype=jnp.int32) // SEQ_DEV
    masking = listed[query_block][:, seq_block].astype(jnp.float32)
    scores = seq_sums * masking
    top_scores = lax.top_k(scores, TOPK)[0]
    return scores, top_scores
```

```python
import functools

import jax
import jax.numpy as jnp
from jax import lax
from jax.experimental import pallas as pl
from jax.experimental.pallas import tpu as pltpu
from jax.sharding import PartitionSpec as P

SEQ_LEN = 64
TOPK = 16
CORES = 2
X_CHIPS = 2
BASIS_SLOTS = 4
LANES = 128


def contract_last(left, right):
    return lax.dot_general(
        left, right, (((1,), (1,)), ((), ())), preferred_element_type=jnp.float32
    )


def ring_kernel(
    n, qa_ref, qg_ref, ba_ref, bg_ref, acts_ref, grads_ref, cand_ref, count_ref,
    scores_ref, top_ref,
    qbuf, bbuf, slot_a, slot_g, acts_v, grads_v, acc_a, acc_g, proj_a, proj_g, seq_all,
    own_sem, basis_sem, token_sem,
    right_sem, left_sem, pair_sem, land_sem, score_send, score_land,
):
    rows, width_a = qa_ref.shape
    width_g = qg_ref.shape[1]
    half = rows // 2
    chips = n // CORES
    z_chips = chips // X_CHIPS
    reach = chips // 2
    me = lax.axis_index("param")
    core = lax.rem(me, CORES)
    chip = lax.div(me, CORES)
    x_pos = lax.rem(chip, X_CHIPS)
    z_pos = lax.div(chip, X_CHIPS)
    pos = z_pos + x_pos * (chips - 1 - 2 * z_pos)
    pair = me + 1 - 2 * core

    def holder(place, which):
        place = lax.rem(place + 2 * chips, chips)
        x = lax.div(place, z_chips)
        z = place + x * (chips - 1 - 2 * place)
        return (z * X_CHIPS + x) * CORES + which

    right = holder(pos + 1, core)
    left = holder(pos - 1, core)

    def source(j):
        turn = j + 2
        k = lax.div(turn, 4)
        t = lax.rem(turn, 4)
        flip = lax.rem(t, 2)
        side = lax.div(t, 2)
        return holder(pos - k + 2 * k * side, core + flip * (1 - 2 * core))

    def basis_copies(j):
        s = source(j)
        place = lax.rem(j, BASIS_SLOTS)
        cols_a = pl.ds(pl.multiple_of(s * width_a, LANES), width_a)
        cols_g = pl.ds(pl.multiple_of(s * width_g, LANES), width_g)
        return (
            pltpu.make_async_copy(ba_ref.at[:, cols_a], slot_a.at[place], basis_sem.at[0, place]),
            pltpu.make_async_copy(bg_ref.at[:, cols_g], slot_g.at[place], basis_sem.at[1, place]),
        )

    own = (
        pltpu.make_async_copy(qa_ref, qbuf.at[me, :, pl.ds(0, width_a)], own_sem.at[0]),
        pltpu.make_async_copy(qg_ref, qbuf.at[me, :, pl.ds(width_a, width_g)], own_sem.at[1]),
    )
    tokens = (
        pltpu.make_async_copy(acts_ref, acts_v, token_sem.at[0]),
        pltpu.make_async_copy(grads_ref, grads_v, token_sem.at[1]),
    )
    for copy in own:
        copy.start()
    for j in range(BASIS_SLOTS):
        for copy in basis_copies(jnp.int32(j)):
            copy.start()
    for copy in tokens:
        copy.start()

    barrier = pltpu.get_barrier_semaphore()

    def greet(j, carry):
        pl.semaphore_signal(
            barrier, inc=1, device_id={"param": lax.rem(me + j, n)},
            device_id_type=pl.DeviceIdType.MESH,
        )
        return carry

    lax.fori_loop(1, n, greet, 0)
    acc_a[...] = jnp.zeros_like(acc_a)
    acc_g[...] = jnp.zeros_like(acc_g)
    proj_a[...] = jnp.zeros_like(proj_a)
    proj_g[...] = jnp.zeros_like(proj_g)
    pl.semaphore_wait(barrier, n - 1)
    for copy in own:
        copy.wait()

    def stage(number, buf, compute):
        sent = []

        def push(s, h, target, sem):
            view = buf.at[s, pl.ds(h * half, half), :]
            return pltpu.make_async_remote_copy(
                src_ref=view, dst_ref=view, send_sem=sem, recv_sem=land_sem.at[number, s, h],
                device_id={"param": target}, device_id_type=pl.DeviceIdType.MESH,
            )

        def send(s, h, target, sem):
            copy = push(s, h, target, sem)
            copy.start()
            sent.append(copy)

        def landed(s, h):
            push(s, h, pair, pair_sem.at[number, 0, 0, h]).wait_recv()

        for h in (0, 1):
            send(me, h, right, right_sem.at[number, 0, h])
            send(me, 1 - h, left, left_sem.at[number, 0, 1 - h])
        for h in (0, 1):
            send(me, h, pair, pair_sem.at[number, 0, 0, h])
        compute(0)
        for h in (0, 1):
            landed(pair, h)
        compute(1)
        for k in range(1, reach):
            back, front = holder(pos - k, core), holder(pos + k, core)
            for h in (0, 1):
                landed(back, h)
                if k < reach - 1 or h == 0:
                    send(back, h, right, right_sem.at[number, k, h])
                landed(front, 1 - h)
                if k < reach - 1 or h == 0:
                    send(front, 1 - h, left, left_sem.at[number, k, 1 - h])
                send(back, h, pair, pair_sem.at[number, 0, k, h])
                send(front, 1 - h, pair, pair_sem.at[number, 1, k, 1 - h])
            for other in (holder(pos - k, 1 - core), holder(pos + k, 1 - core)):
                for h in (0, 1):
                    landed(other, h)

            def body(j, carry):
                compute(j)
                return carry

            lax.fori_loop(4 * k - 2, 4 * k + 2, body, 0)
        far = holder(pos - reach, core)
        for h in (0, 1):
            landed(far, h)
            send(far, h, pair, pair_sem.at[number, 0, reach, h])
        compute(n - 2)
        for h in (0, 1):
            landed(holder(pos - reach, 1 - core), h)
        compute(n - 1)
        return sent

    def rotate(j):
        j = jnp.int32(j)
        s = source(j)
        place = lax.rem(j, BASIS_SLOTS)
        for copy in basis_copies(j):
            copy.wait()
        acc_a[...] += contract_last(qbuf[s, :, :width_a], slot_a[place])
        acc_g[...] += contract_last(qbuf[s, :, width_a:], slot_g[place])

        @pl.when(j + BASIS_SLOTS < n)
        def _():
            for copy in basis_copies(j + BASIS_SLOTS):
                copy.start()

    sent = stage(0, qbuf, rotate)
    bbuf[me, :, :width_a] = acc_a[...].astype(jnp.bfloat16)
    bbuf[me, :, width_a:] = acc_g[...].astype(jnp.bfloat16)

    def project(j):
        s = source(jnp.int32(j))
        cols_a = pl.ds(pl.multiple_of(s * width_a, LANES), width_a)
        cols_g = pl.ds(pl.multiple_of(s * width_g, LANES), width_g)
        proj_a[...] += contract_last(bbuf[s, :, :width_a], acts_v[:, cols_a])
        proj_g[...] += contract_last(bbuf[s, :, width_a:], grads_v[:, cols_g])

    for copy in tokens:
        copy.wait()
    sent += stage(1, bbuf, project)

    queries = scores_ref.shape[0]
    seq_count = scores_ref.shape[1]
    blocks_q, slots_q = cand_ref.shape
    token_sums = (proj_a[...] * proj_g[...]).reshape(queries, rows // queries, -1).sum(axis=1)
    tok_lane = lax.broadcasted_iota(jnp.int32, token_sums.shape, 1)
    lane = lax.broadcasted_iota(jnp.int32, (queries, LANES), 1)
    row = lax.broadcasted_iota(jnp.int32, (queries, LANES), 0)
    tile = jnp.zeros((queries, LANES), jnp.float32)
    for q in range(seq_count):
        inside = (tok_lane >= q * SEQ_LEN) & (tok_lane < (q + 1) * SEQ_LEN)
        total = jnp.sum(jnp.where(inside, token_sums, 0.0), axis=1, keepdims=True)
        tile = jnp.where(lane == q, total, tile)
    masking = jnp.zeros((queries, LANES), jnp.float32)
    per_block = queries // blocks_q
    for b in range(blocks_q):
        named = jnp.float32(0.0)
        for slot in range(slots_q):
            hit = (slot < count_ref[b]) & (cand_ref[b, slot] == me)
            named += jnp.where(hit, 1.0, 0.0)
        chosen = (row >= b * per_block) & (row < (b + 1) * per_block)
        masking = jnp.where(chosen, named, masking)
    tile = tile * masking
    scores_ref[...] = tile[:, :seq_count]
    seq_all[me] = tile

    def score_copy(j, origin):
        return pltpu.make_async_remote_copy(
            src_ref=seq_all.at[origin], dst_ref=seq_all.at[origin],
            send_sem=score_send.at[j], recv_sem=score_land.at[origin],
            device_id={"param": lax.rem(me + j, n)}, device_id_type=pl.DeviceIdType.MESH,
        )

    def give(j, carry):
        score_copy(j, me).start()
        return carry

    def take(j, carry):
        score_copy(j, lax.rem(me + j, n)).wait_recv()
        return carry

    def given(j, carry):
        score_copy(j, me).wait_send()
        return carry

    lax.fori_loop(1, n, give, 0)
    for copy in sent:
        copy.wait_send()
    lax.fori_loop(1, n, take, 0)
    values = jnp.zeros((queries, LANES), jnp.float32)
    for p in range(n):
        part = seq_all[p]
        values += part if p == 0 else pltpu.roll(part, p * seq_count, 1)
    total_seq = n * seq_count
    values = jnp.where(lane < total_seq, values, -jnp.inf)
    rank = jnp.zeros((queries, LANES), jnp.int32)
    for k in range(total_seq):
        rival = values[:, k : k + 1]
        ahead = (rival > values) | ((rival == values) & (lane > k))
        rank += ahead.astype(jnp.int32)
    best = jnp.zeros((queries, LANES), jnp.float32)
    for m in range(TOPK):
        picked = jnp.sum(jnp.where(rank == m, values, 0.0), axis=1, keepdims=True)
        best = jnp.where(lane == m, picked, best)
    top_ref[...] = best[:, :TOPK]
    lax.fori_loop(1, n, given, 0)


def ring_scores(n, basis_a, basis_g, query_a, query_g, acts, grads, cand_blocks, cand_count):
    queries, rank_size, width_a = query_a.shape
    width_g = query_g.shape[2]
    rows = queries * rank_size
    tok_rows = acts.shape[0]
    stride = width_a + width_g
    reach = n // CORES // 2
    anywhere = pl.BlockSpec(memory_space=pl.ANY)
    scalars = pl.BlockSpec(memory_space=pltpu.SMEM)
    whole = pl.BlockSpec(memory_space=pltpu.VMEM)
    dma = pltpu.SemaphoreType.DMA
    flops = 2 * rows * (basis_a.size + basis_g.size + acts.size + grads.size)
    moved = 2 * (basis_a.size + basis_g.size + acts.size + grads.size)
    return pl.pallas_call(
        functools.partial(ring_kernel, n),
        out_shape=(
            jax.ShapeDtypeStruct((queries, tok_rows // SEQ_LEN), jnp.float32),
            jax.ShapeDtypeStruct((queries, TOPK), jnp.float32),
        ),
        in_specs=[anywhere] * 6 + [scalars] * 2,
        out_specs=(whole, whole),
        scratch_shapes=[
            pltpu.VMEM((n, rows, stride), jnp.bfloat16),
            pltpu.VMEM((n, rows, stride), jnp.bfloat16),
            pltpu.VMEM((BASIS_SLOTS, width_a, width_a), jnp.bfloat16),
            pltpu.VMEM((BASIS_SLOTS, width_g, width_g), jnp.bfloat16),
            pltpu.VMEM(acts.shape, jnp.bfloat16),
            pltpu.VMEM(grads.shape, jnp.bfloat16),
            pltpu.VMEM((rows, width_a), jnp.float32),
            pltpu.VMEM((rows, width_g), jnp.float32),
            pltpu.VMEM((rows, tok_rows), jnp.float32),
            pltpu.VMEM((rows, tok_rows), jnp.float32),
            pltpu.VMEM((n, queries, LANES), jnp.float32),
            dma((2,)),
            dma((2, BASIS_SLOTS)),
            dma((2,)),
            dma((2, reach, 2)),
            dma((2, reach, 2)),
            dma((2, 2, reach + 1, 2)),
            dma((2, n, 2)),
            dma((n,)),
            dma((n,)),
        ],
        compiler_params=pltpu.CompilerParams(
            collective_id=0, has_side_effects=True, vmem_limit_bytes=56 * 1024 * 1024
        ),
        cost_estimate=pl.CostEstimate(flops=flops, bytes_accessed=moved, transcendentals=0),
    )(
        query_a.reshape(rows, width_a), query_g.reshape(rows, width_g),
        basis_a, basis_g, acts, grads, cand_blocks, cand_count,
    )


def plain_scores(basis_a, basis_g, query_a, query_g, acts, grads, cand_blocks, cand_count):
    queries, rank_size, width_a = query_a.shape
    width_g = query_g.shape[2]
    rows = queries * rank_size
    stride = width_a + width_g
    tok_rows = acts.shape[0]
    seq_count = tok_rows // SEQ_LEN
    per_block = queries // cand_blocks.shape[0]
    my_index = lax.axis_index("param")

    def whole(part_a, part_g):
        joined = jnp.concatenate([part_a, part_g], axis=1)
        piece = lax.all_gather(joined, "param", axis=1, tiled=True)
        divided = piece.reshape(rows, -1, stride)
        return (
            divided[:, :, :width_a].reshape(rows, -1),
            divided[:, :, width_a:].reshape(rows, -1),
        )

    full_a, full_g = whole(query_a.reshape(rows, width_a), query_g.reshape(rows, width_g))
    back_a = contract_last(full_a, basis_a).astype(jnp.bfloat16)
    back_g = contract_last(full_g, basis_g).astype(jnp.bfloat16)
    full_a, full_g = whole(back_a, back_g)
    products = contract_last(full_a, acts) * contract_last(full_g, grads)
    seq_sums = products.reshape(queries, rank_size, seq_count, SEQ_LEN).sum(axis=(1, 3))
    positions = jnp.arange(cand_blocks.shape[1], dtype=jnp.int32)
    live_slot = positions[None, :] < cand_count[:, None]
    named = jnp.sum((live_slot & (cand_blocks == my_index)).astype(jnp.float32), axis=1)
    scores = seq_sums * jnp.repeat(named, per_block)[:, None]
    every = lax.all_gather(scores, "param", axis=1, tiled=True)
    return scores, lax.top_k(every, TOPK)[0]


def solution(mesh):
    n = mesh.shape["param"]

    def shards(basis_a, basis_g, query_a, query_g, acts, grads, cand_blocks, cand_count):
        args = (basis_a, basis_g, query_a, query_g, acts, grads, cand_blocks, cand_count)
        fits = (
            n % (2 * CORES * X_CHIPS) == 0
            and query_a.shape[2] % LANES == 0
            and query_g.shape[2] % LANES == 0
            and n * (acts.shape[0] // SEQ_LEN) <= LANES
        )
        return ring_scores(n, *args) if fits else plain_scores(*args)

    in_specs = (
        P("param", None),
        P("param", None),
        P("grp", None, "param"),
        P("grp", None, "param"),
        P(("grp", "param"), None),
        P(("grp", "param"), None),
        P("grp", None),
        P("grp"),
    )
    out_specs = (P("grp", "param"), P("grp", None))
    return jax.shard_map(shards, mesh=mesh, in_specs=in_specs, out_specs=out_specs, check_vma=False)
```

```python
import functools

import jax
import jax.numpy as jnp
from jax import lax
from jax.experimental import pallas as pl
from jax.experimental.pallas import tpu as pltpu
from jax.sharding import PartitionSpec as P

SEQ_LEN = 64
TOPK = 16
CORES = 2
X_CHIPS = 2
BASIS_SLOTS = 4
LANES = 128


def contract_last(left, right):
    return lax.dot_general(
        left, right, (((1,), (1,)), ((), ())), preferred_element_type=jnp.float32
    )


def ring_kernel(
    n, qa_ref, qg_ref, ba_ref, bg_ref, acts_ref, grads_ref, cand_ref, count_ref,
    out_ref,
    qa_all, qg_all, ba_all, bg_all, slot_a, slot_g, acts_v, grads_v,
    acc_a, acc_g, proj_a, proj_g, seq_all,
    own_sem, basis_sem, token_sem,
    right_sem, left_sem, pair_sem, land_sem, score_send, score_land,
):
    rows, width_a = qa_ref.shape
    width_g = qg_ref.shape[1]
    half = rows // 2
    chips = n // CORES
    z_chips = chips // X_CHIPS
    reach = chips // 2
    me = lax.axis_index("param")
    core = lax.rem(me, CORES)
    chip = lax.div(me, CORES)
    x_pos = lax.rem(chip, X_CHIPS)
    z_pos = lax.div(chip, X_CHIPS)
    pos = z_pos + x_pos * (chips - 1 - 2 * z_pos)
    pair = me + 1 - 2 * core

    def holder(place, which):
        place = lax.rem(place + 2 * chips, chips)
        x = lax.div(place, z_chips)
        z = place + x * (chips - 1 - 2 * place)
        return (z * X_CHIPS + x) * CORES + which

    right = holder(pos + 1, core)
    left = holder(pos - 1, core)

    def source(j):
        turn = j + 2
        k = lax.div(turn, 4)
        t = lax.rem(turn, 4)
        flip = lax.rem(t, 2)
        side = lax.div(t, 2)
        return holder(pos - k + 2 * k * side, core + flip * (1 - 2 * core))

    def basis_copy(part, j):
        basis_ref, slots, width = ((ba_ref, slot_a, width_a), (bg_ref, slot_g, width_g))[part]
        place = lax.rem(j, BASIS_SLOTS)
        cols = pl.ds(pl.multiple_of(source(j) * width, LANES), width)
        return pltpu.make_async_copy(
            basis_ref.at[:, cols], slots.at[place], basis_sem.at[part, place]
        )

    own = (
        pltpu.make_async_copy(qa_ref, qa_all.at[me], own_sem.at[0]),
        pltpu.make_async_copy(qg_ref, qg_all.at[me], own_sem.at[1]),
    )
    tokens = (
        pltpu.make_async_copy(acts_ref, acts_v, token_sem.at[0]),
        pltpu.make_async_copy(grads_ref, grads_v, token_sem.at[1]),
    )
    for copy in own:
        copy.start()

    barrier = pltpu.get_barrier_semaphore()

    def greet(j, carry):
        pl.semaphore_signal(
            barrier, inc=1, device_id={"param": lax.rem(me + j, n)},
            device_id_type=pl.DeviceIdType.MESH,
        )
        return carry

    lax.fori_loop(1, n, greet, 0)
    for j in range(BASIS_SLOTS):
        for part in (0, 1):
            basis_copy(part, jnp.int32(j)).start()
    for copy in tokens:
        copy.start()
    for total in (acc_a, acc_g, proj_a, proj_g):
        total[...] = jnp.zeros_like(total)
    pl.semaphore_wait(barrier, n - 1)

    sent = []

    def gather(number, buf, compute):
        def push(s, h, target, sem):
            view = buf.at[s, pl.ds(h * half, half), :]
            return pltpu.make_async_remote_copy(
                src_ref=view, dst_ref=view, send_sem=sem, recv_sem=land_sem.at[number, s, h],
                device_id={"param": target}, device_id_type=pl.DeviceIdType.MESH,
            )

        def send(s, h, target, sem):
            copy = push(s, h, target, sem)
            copy.start()
            sent.append(copy)

        def landed(s, h):
            push(s, h, pair, pair_sem.at[number, 0, 0, h]).wait_recv()

        def begin():
            for h in (0, 1):
                send(me, h, right, right_sem.at[number, 0, h])
                send(me, 1 - h, left, left_sem.at[number, 0, 1 - h])
            for h in (0, 1):
                send(me, h, pair, pair_sem.at[number, 0, 0, h])

        def forward(k):
            back, front = holder(pos - k, core), holder(pos + k, core)
            for h in (0, 1):
                if k == reach:
                    landed(back, h)
                    send(back, h, pair, pair_sem.at[number, 0, k, h])
                    continue
                landed(back, h)
                if k < reach - 1 or h == 0:
                    send(back, h, right, right_sem.at[number, k, h])
                landed(front, 1 - h)
                if k < reach - 1 or h == 0:
                    send(front, 1 - h, left, left_sem.at[number, k, 1 - h])
                send(back, h, pair, pair_sem.at[number, 0, k, h])
                send(front, 1 - h, pair, pair_sem.at[number, 1, k, 1 - h])

        def work(k):
            if k in (0, reach):
                first = 0 if k == 0 else n - 2
                compute(jnp.int32(first))
                for h in (0, 1):
                    landed(holder(pos - k, 1 - core), h)
                compute(jnp.int32(first + 1))
                return
            for other in (holder(pos - k, 1 - core), holder(pos + k, 1 - core)):
                for h in (0, 1):
                    landed(other, h)

            def body(j, carry):
                compute(j)
                return carry

            lax.fori_loop(4 * k - 2, 4 * k + 2, body, 0)

        return begin, forward, work

    def rotate(part, query, slots, total):
        def compute(j):
            place = lax.rem(j, BASIS_SLOTS)
            basis_copy(part, j).wait()
            total[...] += contract_last(query[source(j)], slots[place])

            @pl.when(j + BASIS_SLOTS < n)
            def _():
                basis_copy(part, j + BASIS_SLOTS).start()

        return compute

    def project(backs, held, width, total):
        def compute(j):
            s = source(j)
            cols = pl.ds(pl.multiple_of(s * width, LANES), width)
            total[...] += contract_last(backs[s], held[:, cols])

        return compute

    begin_qa, forward_qa, work_qa = gather(0, qa_all, rotate(0, qa_all, slot_a, acc_a))
    begin_qg, forward_qg, work_qg = gather(1, qg_all, rotate(1, qg_all, slot_g, acc_g))
    begin_ba, forward_ba, work_ba = gather(2, ba_all, project(ba_all, acts_v, width_a, proj_a))
    begin_bg, forward_bg, work_bg = gather(3, bg_all, project(bg_all, grads_v, width_g, proj_g))
    last = reach - 1

    own[0].wait()
    begin_qa()
    own[1].wait()
    work_qa(0)
    forward_qa(1)
    begin_qg()
    work_qa(1)
    work_qg(0)
    for k in range(2, last):
        forward_qa(k)
        work_qa(k)
        forward_qg(k - 1)
        work_qg(k - 1)
    forward_qa(last)
    forward_qg(last - 1)
    work_qa(last)
    forward_qa(reach)
    work_qa(reach)
    ba_all[me] = acc_a[...].astype(jnp.bfloat16)
    begin_ba()
    work_qg(last - 1)
    forward_qg(last)
    for copy in tokens:
        copy.wait()
    work_ba(0)
    work_qg(last)
    forward_ba(1)
    forward_qg(reach)
    work_qg(reach)
    bg_all[me] = acc_g[...].astype(jnp.bfloat16)
    begin_bg()
    work_ba(1)
    work_bg(0)
    for k in range(2, last):
        forward_ba(k)
        work_ba(k)
        forward_bg(k - 1)
        work_bg(k - 1)
    forward_ba(last)
    forward_bg(last - 1)
    work_ba(last)
    forward_ba(reach)
    work_ba(reach)
    work_bg(last - 1)
    forward_bg(last)
    work_bg(last)
    forward_bg(reach)
    work_bg(reach)

    queries = seq_all.shape[1]
    seq_count = acts_v.shape[0] // SEQ_LEN
    blocks_q, slots_q = cand_ref.shape
    token_sums = (proj_a[...] * proj_g[...]).reshape(queries, rows // queries, -1).sum(axis=1)
    tok_lane = lax.broadcasted_iota(jnp.int32, token_sums.shape, 1)
    lane = lax.broadcasted_iota(jnp.int32, (queries, LANES), 1)
    row = lax.broadcasted_iota(jnp.int32, (queries, LANES), 0)
    tile = jnp.zeros((queries, LANES), jnp.float32)
    for q in range(seq_count):
        inside = (tok_lane >= q * SEQ_LEN) & (tok_lane < (q + 1) * SEQ_LEN)
        total = jnp.sum(jnp.where(inside, token_sums, 0.0), axis=1, keepdims=True)
        tile = jnp.where(lane == q, total, tile)
    masking = jnp.zeros((queries, LANES), jnp.float32)
    per_block = queries // blocks_q
    for b in range(blocks_q):
        named = jnp.float32(0.0)
        for slot in range(slots_q):
            hit = (slot < count_ref[b]) & (cand_ref[b, slot] == me)
            named += jnp.where(hit, 1.0, 0.0)
        chosen = (row >= b * per_block) & (row < (b + 1) * per_block)
        masking = jnp.where(chosen, named, masking)
    tile = tile * masking
    seq_all[me] = tile

    def score_copy(j, origin):
        return pltpu.make_async_remote_copy(
            src_ref=seq_all.at[origin], dst_ref=seq_all.at[origin],
            send_sem=score_send.at[j], recv_sem=score_land.at[origin],
            device_id={"param": lax.rem(me + j, n)}, device_id_type=pl.DeviceIdType.MESH,
        )

    def give(j, carry):
        score_copy(j, me).start()
        return carry

    def take(j, carry):
        score_copy(j, lax.rem(me + j, n)).wait_recv()
        return carry

    def given(j, carry):
        score_copy(j, me).wait_send()
        return carry

    lax.fori_loop(1, n, give, 0)
    out_ref[:queries, :] = tile
    for copy in sent:
        copy.wait_send()
    lax.fori_loop(1, n, take, 0)
    values = jnp.zeros((queries, LANES), jnp.float32)
    for p in range(n):
        part = seq_all[p]
        values += part if p == 0 else pltpu.roll(part, p * seq_count, 1)
    out_ref[queries:, :] = values
    lax.fori_loop(1, n, given, 0)


def rank_kernel(total_seq, in_ref, scores_ref, top_ref):
    queries, seq_count = scores_ref.shape
    scores_ref[...] = in_ref[:queries, :seq_count]
    lane = lax.broadcasted_iota(jnp.int32, (queries, LANES), 1)
    values = jnp.where(lane < total_seq, in_ref[queries:, :], -jnp.inf)
    rank = jnp.zeros((queries, LANES), jnp.int32)
    for k in range(total_seq):
        rival = values[:, k : k + 1]
        ahead = (rival > values) | ((rival == values) & (lane > k))
        rank += ahead.astype(jnp.int32)
    best = jnp.zeros((queries, LANES), jnp.float32)
    for m in range(TOPK):
        picked = jnp.sum(jnp.where(rank == m, values, 0.0), axis=1, keepdims=True)
        best = jnp.where(lane == m, picked, best)
    top_ref[...] = best[:, :TOPK]


def ring_scores(n, basis_a, basis_g, query_a, query_g, acts, grads, cand_blocks, cand_count):
    queries, rank_size, width_a = query_a.shape
    width_g = query_g.shape[2]
    rows = queries * rank_size
    tok_rows = acts.shape[0]
    reach = n // CORES // 2
    anywhere = pl.BlockSpec(memory_space=pl.ANY)
    scalars = pl.BlockSpec(memory_space=pltpu.SMEM)
    whole = pl.BlockSpec(memory_space=pltpu.VMEM)
    dma = pltpu.SemaphoreType.DMA
    flops = 2 * rows * (basis_a.size + basis_g.size + acts.size + grads.size)
    moved = 2 * (basis_a.size + basis_g.size + acts.size + grads.size)
    seq_count = tok_rows // SEQ_LEN
    gathered = pl.pallas_call(
        functools.partial(ring_kernel, n),
        out_shape=jax.ShapeDtypeStruct((2 * queries, LANES), jnp.float32),
        in_specs=[anywhere] * 6 + [scalars] * 2,
        out_specs=whole,
        scratch_shapes=[
            pltpu.VMEM((n, rows, width_a), jnp.bfloat16),
            pltpu.VMEM((n, rows, width_g), jnp.bfloat16),
            pltpu.VMEM((n, rows, width_a), jnp.bfloat16),
            pltpu.VMEM((n, rows, width_g), jnp.bfloat16),
            pltpu.VMEM((BASIS_SLOTS, width_a, width_a), jnp.bfloat16),
            pltpu.VMEM((BASIS_SLOTS, width_g, width_g), jnp.bfloat16),
            pltpu.VMEM(acts.shape, jnp.bfloat16),
            pltpu.VMEM(grads.shape, jnp.bfloat16),
            pltpu.VMEM((rows, width_a), jnp.float32),
            pltpu.VMEM((rows, width_g), jnp.float32),
            pltpu.VMEM((rows, tok_rows), jnp.float32),
            pltpu.VMEM((rows, tok_rows), jnp.float32),
            pltpu.VMEM((n, queries, LANES), jnp.float32),
            dma((2,)),
            dma((2, BASIS_SLOTS)),
            dma((2,)),
            dma((4, reach, 2)),
            dma((4, reach, 2)),
            dma((4, 2, reach + 1, 2)),
            dma((4, n, 2)),
            dma((n,)),
            dma((n,)),
        ],
        compiler_params=pltpu.CompilerParams(
            collective_id=0, has_side_effects=True, vmem_limit_bytes=56 * 1024 * 1024
        ),
        cost_estimate=pl.CostEstimate(flops=flops, bytes_accessed=moved, transcendentals=0),
    )(
        query_a.reshape(rows, width_a), query_g.reshape(rows, width_g),
        basis_a, basis_g, acts, grads, cand_blocks, cand_count,
    )
    return pl.pallas_call(
        functools.partial(rank_kernel, n * seq_count),
        out_shape=(
            jax.ShapeDtypeStruct((queries, seq_count), jnp.float32),
            jax.ShapeDtypeStruct((queries, TOPK), jnp.float32),
        ),
        in_specs=[whole],
        out_specs=(whole, whole),
    )(gathered)


def plain_scores(basis_a, basis_g, query_a, query_g, acts, grads, cand_blocks, cand_count):
    queries, rank_size, width_a = query_a.shape
    width_g = query_g.shape[2]
    rows = queries * rank_size
    stride = width_a + width_g
    tok_rows = acts.shape[0]
    seq_count = tok_rows // SEQ_LEN
    per_block = queries // cand_blocks.shape[0]
    my_index = lax.axis_index("param")

    def whole(part_a, part_g):
        joined = jnp.concatenate([part_a, part_g], axis=1)
        piece = lax.all_gather(joined, "param", axis=1, tiled=True)
        divided = piece.reshape(rows, -1, stride)
        return (
            divided[:, :, :width_a].reshape(rows, -1),
            divided[:, :, width_a:].reshape(rows, -1),
        )

    full_a, full_g = whole(query_a.reshape(rows, width_a), query_g.reshape(rows, width_g))
    back_a = contract_last(full_a, basis_a).astype(jnp.bfloat16)
    back_g = contract_last(full_g, basis_g).astype(jnp.bfloat16)
    full_a, full_g = whole(back_a, back_g)
    products = contract_last(full_a, acts) * contract_last(full_g, grads)
    seq_sums = products.reshape(queries, rank_size, seq_count, SEQ_LEN).sum(axis=(1, 3))
    positions = jnp.arange(cand_blocks.shape[1], dtype=jnp.int32)
    live_slot = positions[None, :] < cand_count[:, None]
    named = jnp.sum((live_slot & (cand_blocks == my_index)).astype(jnp.float32), axis=1)
    scores = seq_sums * jnp.repeat(named, per_block)[:, None]
    every = lax.all_gather(scores, "param", axis=1, tiled=True)
    return scores, lax.top_k(every, TOPK)[0]


def solution(mesh):
    n = mesh.shape["param"]

    def shards(basis_a, basis_g, query_a, query_g, acts, grads, cand_blocks, cand_count):
        args = (basis_a, basis_g, query_a, query_g, acts, grads, cand_blocks, cand_count)
        fits = (
            n % (2 * CORES * X_CHIPS) == 0
            and n >= 8 * CORES
            and query_a.shape[2] % LANES == 0
            and query_g.shape[2] % LANES == 0
            and n * (acts.shape[0] // SEQ_LEN) <= LANES
        )
        return ring_scores(n, *args) if fits else plain_scores(*args)

    in_specs = (
        P("param", None),
        P("param", None),
        P("grp", None, "param"),
        P("grp", None, "param"),
        P(("grp", "param"), None),
        P(("grp", "param"), None),
        P("grp", None),
        P("grp"),
    )
    out_specs = (P("grp", "param"), P("grp", None))
    return jax.shard_map(shards, mesh=mesh, in_specs=in_specs, out_specs=out_specs, check_vma=False)
```

```python
import functools

import jax
import jax.numpy as jnp
from jax import lax
from jax.experimental import pallas as pl
from jax.experimental.pallas import tpu as pltpu
from jax.sharding import PartitionSpec as P

SEQ_LEN = 64
TOPK = 16
CORES = 2
X_CHIPS = 2
BASIS_SLOTS = 4
LANES = 128


def contract_last(left, right):
    return lax.dot_general(
        left, right, (((1,), (1,)), ((), ())), preferred_element_type=jnp.float32
    )


def ring_kernel(
    n, qa_ref, qg_ref, ba_ref, bg_ref, acts_ref, grads_ref, cand_ref, count_ref,
    out_ref,
    qa_all, qg_all, ba_all, bg_all, slot_a, slot_g, acts_v, grads_v,
    acc_a, acc_g, proj_a, proj_g, plane_all, line_all,
    own_sem, basis_sem, token_sem,
    right_sem, left_sem, pair_sem, land_sem, plane_send, plane_land, line_send, line_land,
):
    rows, width_a = qa_ref.shape
    width_g = qg_ref.shape[1]
    half = rows // 2
    chips = n // CORES
    z_chips = chips // X_CHIPS
    reach = chips // 2
    me = lax.axis_index("param")
    core = lax.rem(me, CORES)
    chip = lax.div(me, CORES)
    x_pos = lax.rem(chip, X_CHIPS)
    z_pos = lax.div(chip, X_CHIPS)
    pos = z_pos + x_pos * (chips - 1 - 2 * z_pos)
    pair = me + 1 - 2 * core

    def holder(place, which):
        place = lax.rem(place + 2 * chips, chips)
        x = lax.div(place, z_chips)
        z = place + x * (chips - 1 - 2 * place)
        return (z * X_CHIPS + x) * CORES + which

    plane = X_CHIPS * CORES
    seat = lax.rem(me, plane)

    def plane_peer(j):
        return z_pos * plane + lax.rem(seat + j, plane)

    def line_peer(j):
        return lax.rem(z_pos + j, z_chips) * plane + seat

    right = holder(pos + 1, core)
    left = holder(pos - 1, core)

    def source(j):
        turn = j + 2
        k = lax.div(turn, 4)
        t = lax.rem(turn, 4)
        flip = lax.rem(t, 2)
        side = lax.div(t, 2)
        return holder(pos - k + 2 * k * side, core + flip * (1 - 2 * core))

    def basis_copy(part, j):
        basis_ref, slots, width = ((ba_ref, slot_a, width_a), (bg_ref, slot_g, width_g))[part]
        place = lax.rem(j, BASIS_SLOTS)
        cols = pl.ds(pl.multiple_of(source(j) * width, LANES), width)
        return pltpu.make_async_copy(
            basis_ref.at[:, cols], slots.at[place], basis_sem.at[part, place]
        )

    own = (
        pltpu.make_async_copy(qa_ref, qa_all.at[me], own_sem.at[0]),
        pltpu.make_async_copy(qg_ref, qg_all.at[me], own_sem.at[1]),
    )
    tokens = (
        pltpu.make_async_copy(acts_ref, acts_v, token_sem.at[0]),
        pltpu.make_async_copy(grads_ref, grads_v, token_sem.at[1]),
    )
    for copy in own:
        copy.start()

    barrier = pltpu.get_barrier_semaphore()

    for peer, count in ((plane_peer, plane), (line_peer, z_chips)):
        for j in range(1, count):
            pl.semaphore_signal(
                barrier, inc=1, device_id={"param": peer(j)},
                device_id_type=pl.DeviceIdType.MESH,
            )
    for j in range(BASIS_SLOTS):
        for part in (0, 1):
            basis_copy(part, jnp.int32(j)).start()
    for copy in tokens:
        copy.start()
    for total in (acc_a, acc_g, proj_a, proj_g):
        total[...] = jnp.zeros_like(total)
    pl.semaphore_wait(barrier, plane + z_chips - 2)

    sent = []

    def gather(number, buf, compute):
        def push(s, h, target, sem):
            view = buf.at[s, pl.ds(h * half, half), :]
            return pltpu.make_async_remote_copy(
                src_ref=view, dst_ref=view, send_sem=sem, recv_sem=land_sem.at[number, s, h],
                device_id={"param": target}, device_id_type=pl.DeviceIdType.MESH,
            )

        def send(s, h, target, sem):
            copy = push(s, h, target, sem)
            copy.start()
            sent.append(copy)

        def landed(s, h):
            push(s, h, pair, pair_sem.at[number, 0, 0, h]).wait_recv()

        def begin():
            for h in (0, 1):
                send(me, h, right, right_sem.at[number, 0, h])
                send(me, 1 - h, left, left_sem.at[number, 0, 1 - h])
            for h in (0, 1):
                send(me, h, pair, pair_sem.at[number, 0, 0, h])

        def forward(k):
            back, front = holder(pos - k, core), holder(pos + k, core)
            for h in (0, 1):
                if k == reach:
                    landed(back, h)
                    send(back, h, pair, pair_sem.at[number, 0, k, h])
                    continue
                landed(back, h)
                if k < reach - 1 or h == 0:
                    send(back, h, right, right_sem.at[number, k, h])
                landed(front, 1 - h)
                if k < reach - 1 or h == 0:
                    send(front, 1 - h, left, left_sem.at[number, k, 1 - h])
                send(back, h, pair, pair_sem.at[number, 0, k, h])
                send(front, 1 - h, pair, pair_sem.at[number, 1, k, 1 - h])

        def work(k):
            if k in (0, reach):
                first = 0 if k == 0 else n - 2
                compute(jnp.int32(first))
                for h in (0, 1):
                    landed(holder(pos - k, 1 - core), h)
                compute(jnp.int32(first + 1))
                return
            for other in (holder(pos - k, 1 - core), holder(pos + k, 1 - core)):
                for h in (0, 1):
                    landed(other, h)

            def body(j, carry):
                compute(j)
                return carry

            lax.fori_loop(4 * k - 2, 4 * k + 2, body, 0)

        return begin, forward, work

    def rotate(part, query, slots, total):
        def compute(j):
            place = lax.rem(j, BASIS_SLOTS)
            basis_copy(part, j).wait()
            total[...] += contract_last(query[source(j)], slots[place])

            @pl.when(j + BASIS_SLOTS < n)
            def _():
                basis_copy(part, j + BASIS_SLOTS).start()

        return compute

    def project(backs, held, width, total):
        def compute(j):
            s = source(j)
            cols = pl.ds(pl.multiple_of(s * width, LANES), width)
            total[...] += contract_last(backs[s], held[:, cols])

        return compute

    begin_qa, forward_qa, work_qa = gather(0, qa_all, rotate(0, qa_all, slot_a, acc_a))
    begin_qg, forward_qg, work_qg = gather(1, qg_all, rotate(1, qg_all, slot_g, acc_g))
    begin_ba, forward_ba, work_ba = gather(2, ba_all, project(ba_all, acts_v, width_a, proj_a))
    begin_bg, forward_bg, work_bg = gather(3, bg_all, project(bg_all, grads_v, width_g, proj_g))
    last = reach - 1

    own[0].wait()
    begin_qa()
    own[1].wait()
    work_qa(0)
    forward_qa(1)
    begin_qg()
    work_qa(1)
    work_qg(0)
    for k in range(2, last):
        forward_qa(k)
        work_qa(k)
        forward_qg(k - 1)
        work_qg(k - 1)
    forward_qa(last)
    forward_qg(last - 1)
    work_qa(last)
    forward_qa(reach)
    work_qa(reach)
    ba_all[me] = acc_a[...].astype(jnp.bfloat16)
    begin_ba()
    work_qg(last - 1)
    forward_qg(last)
    for copy in tokens:
        copy.wait()
    work_ba(0)
    work_qg(last)
    forward_ba(1)
    forward_qg(reach)
    work_qg(reach)
    bg_all[me] = acc_g[...].astype(jnp.bfloat16)
    begin_bg()
    work_ba(1)
    work_bg(0)
    for k in range(2, last):
        forward_ba(k)
        work_ba(k)
        forward_bg(k - 1)
        work_bg(k - 1)
    forward_ba(last)
    forward_bg(last - 1)
    work_ba(last)
    forward_ba(reach)
    work_ba(reach)
    work_bg(last - 1)
    settled = len(sent)
    forward_bg(last)
    work_bg(last)
    for copy in sent[:settled]:
        copy.wait_send()
    forward_bg(reach)
    work_bg(reach)

    queries = plane_all.shape[1]
    seq_count = acts_v.shape[0] // SEQ_LEN
    blocks_q, slots_q = cand_ref.shape
    token_sums = (proj_a[...] * proj_g[...]).reshape(queries, rows // queries, -1).sum(axis=1)
    tok_lane = lax.broadcasted_iota(jnp.int32, token_sums.shape, 1)
    lane = lax.broadcasted_iota(jnp.int32, (queries, LANES), 1)
    row = lax.broadcasted_iota(jnp.int32, (queries, LANES), 0)
    tile = jnp.zeros((queries, LANES), jnp.float32)
    for q in range(seq_count):
        inside = (tok_lane >= q * SEQ_LEN) & (tok_lane < (q + 1) * SEQ_LEN)
        total = jnp.sum(jnp.where(inside, token_sums, 0.0), axis=1, keepdims=True)
        tile = jnp.where(lane == q, total, tile)
    masking = jnp.zeros((queries, LANES), jnp.float32)
    per_block = queries // blocks_q
    for b in range(blocks_q):
        named = jnp.float32(0.0)
        for slot in range(slots_q):
            hit = (slot < count_ref[b]) & (cand_ref[b, slot] == me)
            named += jnp.where(hit, 1.0, 0.0)
        chosen = (row >= b * per_block) & (row < (b + 1) * per_block)
        masking = jnp.where(chosen, named, masking)
    tile = tile * masking
    out_ref[:queries, :] = tile

    def exchange(everyone, mine, count, peer, send_sem, recv_sem, step):
        copies = []
        for j in range(1, count):
            copy = pltpu.make_async_remote_copy(
                src_ref=everyone.at[mine], dst_ref=everyone.at[mine],
                send_sem=send_sem.at[j], recv_sem=recv_sem.at[mine],
                device_id={"param": peer(j)}, device_id_type=pl.DeviceIdType.MESH,
            )
            copy.start()
            copies.append(copy)
        for j in range(1, count):
            origin = lax.rem(mine + j, count)
            pltpu.make_async_remote_copy(
                src_ref=everyone.at[origin], dst_ref=everyone.at[origin],
                send_sem=send_sem.at[j], recv_sem=recv_sem.at[origin],
                device_id={"param": peer(j)}, device_id_type=pl.DeviceIdType.MESH,
            ).wait_recv()
        merged = everyone[0]
        for p in range(1, count):
            merged += pltpu.roll(everyone[p], p * step, 1)
        return merged, copies

    plane_all[seat] = tile
    merged, plane_sent = exchange(
        plane_all, seat, plane, plane_peer, plane_send, plane_land, seq_count
    )
    line_all[z_pos] = merged
    merged, line_sent = exchange(
        line_all, z_pos, z_chips, line_peer, line_send, line_land, plane * seq_count
    )
    out_ref[queries:, :] = merged
    for copy in sent[settled:] + plane_sent + line_sent:
        copy.wait_send()


def rank_kernel(total_seq, in_ref, scores_ref, top_ref):
    seq_count, queries = scores_ref.shape
    scores_ref[...] = in_ref[:queries, :].T[:seq_count, :]
    lane = lax.broadcasted_iota(jnp.int32, (queries, LANES), 1)
    values = jnp.where(lane < total_seq, in_ref[queries:, :], -jnp.inf)
    rank = jnp.zeros((queries, LANES), jnp.int32)
    for k in range(total_seq):
        rival = values[:, k : k + 1]
        ahead = (rival > values) | ((rival == values) & (lane > k))
        rank += ahead.astype(jnp.int32)
    best = jnp.zeros((queries, LANES), jnp.float32)
    for m in range(TOPK):
        picked = jnp.sum(jnp.where(rank == m, values, 0.0), axis=1, keepdims=True)
        best = jnp.where(lane == m, picked, best)
    top_ref[...] = best[:, :TOPK]


def ring_scores(n, basis_a, basis_g, query_a, query_g, acts, grads, cand_blocks, cand_count):
    queries, rank_size, width_a = query_a.shape
    width_g = query_g.shape[2]
    rows = queries * rank_size
    tok_rows = acts.shape[0]
    reach = n // CORES // 2
    anywhere = pl.BlockSpec(memory_space=pl.ANY)
    scalars = pl.BlockSpec(memory_space=pltpu.SMEM)
    whole = pl.BlockSpec(memory_space=pltpu.VMEM)
    dma = pltpu.SemaphoreType.DMA
    flops = 2 * rows * (basis_a.size + basis_g.size + acts.size + grads.size)
    moved = 2 * (basis_a.size + basis_g.size + acts.size + grads.size)
    seq_count = tok_rows // SEQ_LEN
    plane = X_CHIPS * CORES
    gathered = pl.pallas_call(
        functools.partial(ring_kernel, n),
        out_shape=jax.ShapeDtypeStruct((2 * queries, LANES), jnp.float32),
        in_specs=[anywhere] * 6 + [scalars] * 2,
        out_specs=whole,
        scratch_shapes=[
            pltpu.VMEM((n, rows, width_a), jnp.bfloat16),
            pltpu.VMEM((n, rows, width_g), jnp.bfloat16),
            pltpu.VMEM((n, rows, width_a), jnp.bfloat16),
            pltpu.VMEM((n, rows, width_g), jnp.bfloat16),
            pltpu.VMEM((BASIS_SLOTS, width_a, width_a), jnp.bfloat16),
            pltpu.VMEM((BASIS_SLOTS, width_g, width_g), jnp.bfloat16),
            pltpu.VMEM(acts.shape, jnp.bfloat16),
            pltpu.VMEM(grads.shape, jnp.bfloat16),
            pltpu.VMEM((rows, width_a), jnp.float32),
            pltpu.VMEM((rows, width_g), jnp.float32),
            pltpu.VMEM((rows, tok_rows), jnp.float32),
            pltpu.VMEM((rows, tok_rows), jnp.float32),
            pltpu.VMEM((plane, queries, LANES), jnp.float32),
            pltpu.VMEM((n // plane, queries, LANES), jnp.float32),
            dma((2,)),
            dma((2, BASIS_SLOTS)),
            dma((2,)),
            dma((4, reach, 2)),
            dma((4, reach, 2)),
            dma((4, 2, reach + 1, 2)),
            dma((4, n, 2)),
            dma((plane,)),
            dma((plane,)),
            dma((n // plane,)),
            dma((n // plane,)),
        ],
        compiler_params=pltpu.CompilerParams(
            collective_id=0, has_side_effects=True, vmem_limit_bytes=56 * 1024 * 1024
        ),
        cost_estimate=pl.CostEstimate(flops=flops, bytes_accessed=moved, transcendentals=0),
    )(
        query_a.reshape(rows, width_a), query_g.reshape(rows, width_g),
        basis_a, basis_g, acts, grads, cand_blocks, cand_count,
    )
    scores, top_scores = pl.pallas_call(
        functools.partial(rank_kernel, n * seq_count),
        out_shape=(
            jax.ShapeDtypeStruct((seq_count, queries), jnp.float32),
            jax.ShapeDtypeStruct((queries, TOPK), jnp.float32),
        ),
        in_specs=[whole],
        out_specs=(whole, whole),
    )(gathered)
    return scores.T, top_scores


def plain_scores(basis_a, basis_g, query_a, query_g, acts, grads, cand_blocks, cand_count):
    queries, rank_size, width_a = query_a.shape
    width_g = query_g.shape[2]
    rows = queries * rank_size
    stride = width_a + width_g
    tok_rows = acts.shape[0]
    seq_count = tok_rows // SEQ_LEN
    per_block = queries // cand_blocks.shape[0]
    my_index = lax.axis_index("param")

    def whole(part_a, part_g):
        joined = jnp.concatenate([part_a, part_g], axis=1)
        piece = lax.all_gather(joined, "param", axis=1, tiled=True)
        divided = piece.reshape(rows, -1, stride)
        return (
            divided[:, :, :width_a].reshape(rows, -1),
            divided[:, :, width_a:].reshape(rows, -1),
        )

    full_a, full_g = whole(query_a.reshape(rows, width_a), query_g.reshape(rows, width_g))
    back_a = contract_last(full_a, basis_a).astype(jnp.bfloat16)
    back_g = contract_last(full_g, basis_g).astype(jnp.bfloat16)
    full_a, full_g = whole(back_a, back_g)
    products = contract_last(full_a, acts) * contract_last(full_g, grads)
    seq_sums = products.reshape(queries, rank_size, seq_count, SEQ_LEN).sum(axis=(1, 3))
    positions = jnp.arange(cand_blocks.shape[1], dtype=jnp.int32)
    live_slot = positions[None, :] < cand_count[:, None]
    named = jnp.sum((live_slot & (cand_blocks == my_index)).astype(jnp.float32), axis=1)
    scores = seq_sums * jnp.repeat(named, per_block)[:, None]
    every = lax.all_gather(scores, "param", axis=1, tiled=True)
    return scores, lax.top_k(every, TOPK)[0]


def solution(mesh):
    n = mesh.shape["param"]

    def shards(basis_a, basis_g, query_a, query_g, acts, grads, cand_blocks, cand_count):
        args = (basis_a, basis_g, query_a, query_g, acts, grads, cand_blocks, cand_count)
        fits = (
            n % (2 * CORES * X_CHIPS) == 0
            and n >= 8 * CORES
            and query_a.shape[2] % LANES == 0
            and query_g.shape[2] % LANES == 0
            and n * (acts.shape[0] // SEQ_LEN) <= LANES
        )
        return ring_scores(n, *args) if fits else plain_scores(*args)

    in_specs = (
        P("param", None),
        P("param", None),
        P("grp", None, "param"),
        P("grp", None, "param"),
        P(("grp", "param"), None),
        P(("grp", "param"), None),
        P("grp", None),
        P("grp"),
    )
    out_specs = (P("grp", "param"), P("grp", None))
    return jax.shard_map(shards, mesh=mesh, in_specs=in_specs, out_specs=out_specs, check_vma=False)
```
